512 devices in a mesh: layer: 8 (over z_lo), lat: 64 (over x, z_hi, y, core).
Axes of the slice: x: 4, y: 4, z: 16 (z_hi: 2, z_lo: 8; z = z_hi * 8 + z_lo), core: 2. Of those that a mesh axis runs over, the one named last changes fastest.
Arguments:
- activations: bfloat16 [512, 9216], P('lat', 'layer'), may hold values from -6 to 6
- enc_weight: bfloat16 [9216, 32768], P('layer', 'lat'), may hold values from -0.0625 to 0.0625
- enc_bias: float32 [32768], P('lat'), may hold values from -3 to 3
- dec_weight: bfloat16 [32768, 9216], P('lat', 'layer'), as said below
- dec_bias: float32 [9216], P('layer'), may hold values from -3 to 3
Outputs:
- enc_grad: bfloat16 [9216, 32768], P('layer', 'lat')
- dec_grad: bfloat16 [32768, 9216], P('lat', 'layer')
The draws below stay inside these ranges and needn't reach their ends.
Inputs may be any that keep to these rules, and one draw needn't show every extreme that they name: `dec_weight`: entries within 24 / sqrt(32768) in magnitude.
All inputs are finite; a program needn't handle non-finite values.
Results may differ from the reference program's by a relative error of at most 0.0075.
Values may be sent and summed in bfloat16 or wider, within the bound.
No kernel may reach another device: no remote copies, remote signals or barrier semaphores. Data moves between devices by JAX's collectives and lax.ppermute only.
A program may use at most 64 MiB of HBM per device.

```python
import math
import jax
import jax.numpy as jnp
from jax import lax

H = 32768
ROWS = 512
LD = 9216


def draw_dec_weight(key, part):
    key = jax.random.fold_in(key, 7)
    base_key, row_key, col_key = jax.random.split(key, 3)
    base = jnp.clip(jax.random.normal(base_key, (H, LD), jnp.float32), -4.0, 4.0)
    row_scale = jnp.exp(jax.random.uniform(row_key, (H, 1), jnp.float32, math.log(0.3), math.log(3.0)))
    col_scale = jnp.exp(jax.random.uniform(col_key, (1, LD), jnp.float32, math.log(0.5), math.log(2.0)))
    return (base * row_scale * col_scale / math.sqrt(H)).astype(jnp.bfloat16)


def shard_levels(stream_key, extent, cuts, low, high):
    def one(axis_at, shards_of):
        steps = jax.random.uniform(jax.random.fold_in(jax.random.fold_in(stream_key, 6), axis_at), (shards_of,), jnp.float32, low / len(cuts), high / len(cuts))
        return jnp.repeat(jnp.exp(steps), extent[axis_at] // shards_of).reshape((-1,) + (1,) * (len(extent) - axis_at - 1))

    loudness = one(*cuts[0])
    for cut in cuts[1:]:
        loudness = loudness * one(*cut)
    return loudness


def gaussian(key, dims, deviation, limit, shards=(), held_as=jnp.bfloat16):
    factor_of = shard_levels(key, dims, shards, -0.22, 0.18) if shards else 1.0
    result = jax.random.normal(key, dims, jnp.float32) * deviation * factor_of
    return jnp.minimum(jnp.maximum(result, -limit), limit).astype(held_as)


def setup_inputs(seed: int = 0) -> dict:
    splits = jax.random.split(jax.random.key(seed), 6)
    return {
        "activations": gaussian(splits[0], (ROWS, LD), 1.0, 6.0, ((0, 64), (1, 8))),
        "enc_weight": gaussian(splits[1], (LD, H), LD ** -0.5, 0.0625, ((0, 8), (1, 64))),
        "enc_bias": gaussian(splits[2], (H,), 0.5, 3.0, ((0, 64),), jnp.float32),
        "dec_weight": draw_dec_weight(jax.random.fold_in(splits[5], 71), 0),
        "dec_bias": gaussian(splits[4], (LD,), 0.5, 3.0, ((0, 8),), jnp.float32),
    }


norm_eps = 1e-06
sparsity = 0.5
sharpness = 4.0

def reference(activations, enc_weight, enc_bias, dec_weight, dec_bias):
    preact = jnp.dot(activations, enc_weight, preferred_element_type=jnp.float32) + enc_bias.astype(jnp.float32)
    dec_f32 = dec_weight.astype(jnp.float32)
    dec_norm = jnp.sqrt(lax.optimization_barrier(jnp.sum(dec_f32 * dec_f32, axis=1)) + norm_eps)
    gating = jax.nn.sigmoid(sharpness * preact)
    latents = (preact * gating).astype(jnp.bfloat16)
    rebuilt = jnp.dot(latents, dec_weight, preferred_element_type=jnp.float32)
    residual = (rebuilt + dec_bias.astype(jnp.float32) - activations.astype(jnp.float32)).astype(jnp.bfloat16)
    lat_sums = lax.optimization_barrier(jnp.sum(latents.astype(jnp.float32), axis=0))
    dec_grad = jnp.dot(latents.T, residual, preferred_element_type=jnp.float32)
    dec_grad = dec_grad + sparsity * lat_sums[:, None] * dec_f32 / dec_norm[:, None]
    lat_grad = jnp.dot(residual, dec_weight.T, preferred_element_type=jnp.float32) + sparsity * dec_norm
    pre_grad = (lat_grad * (gating + sharpness * preact * gating * (1.0 - gating))).astype(jnp.bfloat16)
    enc_grad = jnp.dot(activations.T, pre_grad, preferred_element_type=jnp.float32)
    return (enc_grad.astype(jnp.bfloat16), dec_grad.astype(jnp.bfloat16))
```

```python
import jax
import jax.numpy as jnp
from jax import lax
from jax.sharding import Mesh
from jax.sharding import PartitionSpec as P

norm_eps = 1e-06
sparsity = 0.5
sharpness = 4.0
bf16, f32 = jnp.bfloat16, jnp.float32

LAYER = ("la", "lb", "lc")
LAT = ("x", "zhi", "y", "core")
PLANE = ("x", "y")
SWAP = ((0, 1), (1, 0))


def swap(x, axis):
    return lax.ppermute(x, axis, SWAP)


def spread(block, plane):
    return lax.all_to_all(
        jnp.broadcast_to(block[None], (plane, *block.shape)), PLANE, 0, 0, tiled=True
    )


def pick(x, at, axis):
    return lax.dynamic_index_in_dim(x, at, axis, keepdims=False)


def in_order(mine, other, at, axis):
    first = jnp.where(at == 0, mine, other)
    second = jnp.where(at == 0, other, mine)
    return jnp.stack([first, second], axis=axis)


def split_sum(value):
    high = lax.reduce_precision(value, 8, 7)
    return jnp.stack([high, value - high], axis=0).astype(bf16)


def sum_over_layer(left, right, plane, rows, extra=None):
    lb, lc = lax.axis_index("lb"), lax.axis_index("lc")
    left = left.reshape(2, plane * 2 * rows, -1)

    def part(at):
        return jnp.dot(pick(left, at, 0), right, preferred_element_type=f32)

    def exchange(sent, axis, extra):
        shape = sent.shape
        sent = sent.reshape(-1, shape[-1]).astype(bf16)
        count = sent.shape[0]
        if extra is not None:
            tail = jnp.pad(split_sum(extra), ((0, 14), (0, 0)))
            sent = jnp.concatenate([sent, tail], axis=0)
        got = swap(sent, axis)
        if extra is not None:
            extra = extra + jnp.sum(got[count : count + 2].astype(f32), axis=0)
        return got[:count].astype(f32).reshape(shape), extra

    sent, kept = part(1 - lc), part(lc)
    got, extra = exchange(sent, "lc", extra)
    total = (kept + got).reshape(plane, 2, rows, -1)
    got, extra = exchange(pick(total, 1 - lb, 1), "lb", extra)
    total = pick(total, lb, 1) + got
    got, extra = exchange(total, "la", extra)
    return total + got, extra


def gather_over_layer(block):
    lb, lc = lax.axis_index("lb"), lax.axis_index("lc")
    half = in_order(block, swap(block, "lb"), lb, 1)
    return in_order(half, swap(half, "lc"), lc, 0).reshape(-1, block.shape[-1])


def gather_over_plane_and_core(block, plane):
    mine = spread(block, plane).reshape(-1, block.shape[-1])
    return jnp.concatenate([mine, swap(mine, "core")], axis=0)


def local(activations, enc_weight, enc_bias, dec_weight, dec_bias):
    rows, features = activations.shape
    plane = lax.axis_size("x") * lax.axis_size("y")
    both = jnp.concatenate([activations, swap(activations, "zhi")], axis=0)
    all_rows = gather_over_plane_and_core(both, plane)

    dec_f32 = dec_weight.astype(f32)
    squares = jnp.sum(dec_f32 * dec_f32, axis=1)
    preact, summed_sq = sum_over_layer(all_rows, enc_weight, plane, rows, squares)
    preact = preact + enc_bias
    dec_norm = jnp.sqrt(summed_sq + norm_eps)
    gating = jax.nn.sigmoid(sharpness * preact)
    latents = gather_over_layer((preact * gating).astype(bf16))

    half = plane * 2 * rows
    sent = jnp.dot(latents[half:], dec_weight, preferred_element_type=f32).astype(bf16)
    kept = jnp.dot(latents[:half], dec_weight, preferred_element_type=f32)
    part = (kept + swap(sent, "core").astype(f32)).astype(bf16)
    parts = lax.all_to_all(part.reshape(plane, 2 * rows, features), PLANE, 0, 0, tiled=True)
    part = jnp.sum(parts.astype(f32), axis=0)
    got = swap(part.astype(bf16), "zhi").astype(f32)
    rebuilt = part + jnp.concatenate([got[rows:], got[:rows]], axis=0)
    residual = (rebuilt + dec_bias - both.astype(f32)).astype(bf16)
    residual = gather_over_plane_and_core(residual, plane)

    lat_grad, _ = sum_over_layer(residual, dec_weight.T, plane, rows)
    lat_sums = jnp.sum(latents.astype(f32), axis=0)
    dec_grad = lax.dot_general(
        latents, residual, (((0,), (0,)), ((), ())), preferred_element_type=f32
    )
    dec_grad = dec_grad + (sparsity * lat_sums / dec_norm)[:, None] * dec_f32
    lat_grad = lat_grad + sparsity * dec_norm
    pre_grad = (lat_grad * (gating + sharpness * preact * gating * (1.0 - gating))).astype(bf16)
    pre_grad = gather_over_layer(pre_grad)
    enc_grad = lax.dot_general(
        all_rows, pre_grad, (((0,), (0,)), ((), ())), preferred_element_type=f32
    )
    return (enc_grad.astype(bf16), dec_grad.astype(bf16))


def solution(mesh):
    fine = Mesh(mesh.devices.reshape(2, 2, 2, 4, 2, 4, 2), (*LAYER, *LAT))
    return jax.shard_map(
        local,
        mesh=fine,
        in_specs=(P(LAT, LAYER), P(LAYER, LAT), P(LAT), P(LAT, LAYER), P(LAYER)),
        out_specs=(P(LAYER, LAT), P(LAT, LAYER)),
        check_vma=False,
    )
```

```python
import jax
import jax.numpy as jnp
from jax import lax
from jax.sharding import Mesh
from jax.sharding import PartitionSpec as P

norm_eps = 1e-06
sparsity = 0.5
sharpness = 4.0
bf16, f32 = jnp.bfloat16, jnp.float32

LAYER = ("la", "lb", "lc")
LAT = ("x", "zhi", "y", "core")
PLANE = ("x", "y")
SWAP = ((0, 1), (1, 0))

QUARTER = ("lc", "lb")


def swap(x, axis):
    return lax.ppermute(x, axis, SWAP)


def spread(block, plane):
    blocks = jnp.broadcast_to(block[None], (plane, *block.shape))
    return lax.all_to_all(blocks, PLANE, 0, 0, tiled=True).reshape(-1, block.shape[-1])


def in_order(mine, other, at):
    first = jnp.where(at == 0, mine, other)
    second = jnp.where(at == 0, other, mine)
    return jnp.concatenate([first, second], axis=0)


def dot(a, b, dims=((1,), (0,))):
    return lax.dot_general(a, b, (dims, ((), ())), preferred_element_type=f32)


def sum_over_layer(halves, extra=None):
    parts = jnp.concatenate([h.astype(bf16) for h in halves], axis=0).reshape(4, -1, halves[0].shape[-1])
    count = parts.shape[1]
    if extra is not None:
        tail = jnp.broadcast_to(extra.astype(bf16), (4, 8, *extra.shape))
        parts = jnp.concatenate([parts, tail], axis=1)
    total = jnp.sum(lax.all_to_all(parts, QUARTER, 0, 0, tiled=True).astype(f32), axis=0)
    total = total + swap(total.astype(bf16), "la").astype(f32)
    return (total[:count], total[count]) if extra is not None else total


def gather_over_layer(block):
    half = in_order(block, swap(block, "lb"), lax.axis_index("lb"))
    return half, swap(half, "lc")


def local(activations, enc_weight, enc_bias, dec_weight, dec_bias):
    rows, features = activations.shape
    plane = lax.axis_size("x") * lax.axis_size("y")
    lc = lax.axis_index("lc")

    def at(pair, index):
        return lax.dynamic_index_in_dim(jnp.stack(pair, axis=0), index, 0, keepdims=False)

    both = jnp.concatenate([activations, swap(activations, "zhi")], axis=0)
    near = spread(both, plane)
    acts = (near, swap(near, "core"))

    dec_f32 = dec_weight.astype(f32)
    squares = jnp.sum(dec_f32 * dec_f32, axis=1)
    preact, summed_sq = sum_over_layer([dot(a, enc_weight) for a in acts], squares)
    preact = preact + enc_bias
    dec_norm = jnp.sqrt(summed_sq + norm_eps)
    gating = jax.nn.sigmoid(sharpness * preact)
    latents, far_latents = gather_over_layer((preact * gating).astype(bf16))

    here, there = dot(latents, dec_weight), dot(far_latents, dec_weight)
    sent = jnp.where(lc == 1, here, there).astype(bf16)
    part = (jnp.where(lc == 1, there, here) + swap(sent, "core").astype(f32)).astype(bf16)
    parts = lax.all_to_all(part.reshape(plane, 2 * rows, features), PLANE, 0, 0, tiled=True)
    part = jnp.sum(parts.astype(f32), axis=0)
    got = swap(part.astype(bf16), "zhi").astype(f32)
    rebuilt = part + jnp.concatenate([got[rows:], got[:rows]], axis=0)
    near = spread((rebuilt + dec_bias - both.astype(f32)).astype(bf16), plane)
    residual = (near, swap(near, "core"))

    lat_grad = sum_over_layer([dot(r, dec_weight, ((1,), (1,))) for r in residual])
    lat_sums = jnp.sum(latents.astype(f32), axis=0) + jnp.sum(far_latents.astype(f32), axis=0)
    dec_grad = dot(latents, at(residual, lc), ((0,), (0,)))
    dec_grad = dec_grad + dot(far_latents, at(residual, 1 - lc), ((0,), (0,)))
    dec_grad = dec_grad + (sparsity * lat_sums / dec_norm)[:, None] * dec_f32
    lat_grad = lat_grad + sparsity * dec_norm
    pre_grad = (lat_grad * (gating + sharpness * preact * gating * (1.0 - gating))).astype(bf16)
    pre_grad, far_grad = gather_over_layer(pre_grad)
    enc_grad = dot(at(acts, 1 - lc), far_grad, ((0,), (0,)))
    enc_grad = enc_grad + dot(at(acts, lc), pre_grad, ((0,), (0,)))
    return (enc_grad.astype(bf16), dec_grad.astype(bf16))


def solution(mesh):
    fine = Mesh(mesh.devices.reshape(2, 2, 2, 4, 2, 4, 2), (*LAYER, *LAT))
    return jax.shard_map(
        local,
        mesh=fine,
        in_specs=(P(LAT, LAYER), P(LAYER, LAT), P(LAT), P(LAT, LAYER), P(LAYER)),
        out_specs=(P(LAYER, LAT), P(LAT, LAYER)),
        check_vma=False,
    )
```

```python
import jax
import jax.numpy as jnp
from jax import lax
from jax.sharding import Mesh
from jax.sharding import PartitionSpec as P

norm_eps = 1e-06
sparsity = 0.5
sharpness = 4.0
bf16, f32 = jnp.bfloat16, jnp.float32

LAYER = ("la", "lb", "lc")
LAT = ("x", "zhi", "y", "core")
PLANE = ("x", "y")
SWAP = ((0, 1), (1, 0))

QUARTER = ("lc", "lb")


def swap(x, axis):
    return lax.ppermute(x, axis, SWAP)


def spread(block, plane):
    blocks = jnp.broadcast_to(block[None], (plane, *block.shape))
    return lax.all_to_all(blocks, PLANE, 0, 0, tiled=True).reshape(-1, block.shape[-1])


def in_order(mine, other, at, axis):
    first = jnp.where(at == 0, mine, other)
    second = jnp.where(at == 0, other, mine)
    return jnp.concatenate([first, second], axis=axis)


def dot(a, b, dims=((1,), (0,))):
    return lax.dot_general(a, b, (dims, ((), ())), preferred_element_type=f32)


def sum_over_layer(sides, tail=None):
    parts = [s.astype(bf16).reshape(4, -1, s.shape[-1]) for s in sides]
    if tail is not None:
        parts.append(jnp.broadcast_to(tail.astype(bf16), (4, *tail.shape)))
    parts = jnp.concatenate(parts, axis=1)
    total = jnp.sum(lax.all_to_all(parts, QUARTER, 0, 0, tiled=True).astype(f32), axis=0)
    return total + swap(total.astype(bf16), "la").astype(f32)


def gather_over_layer(block):
    half = in_order(block, swap(block, "lb"), lax.axis_index("lb"), 1)
    return half, swap(half, "lc")


def local(activations, enc_weight, enc_bias, dec_weight, dec_bias):
    rows, features = activations.shape
    plane = lax.axis_size("x") * lax.axis_size("y")
    lc = lax.axis_index("lc")
    count = plane * 2 * rows

    both = jnp.concatenate([activations, swap(activations, "zhi")], axis=0)
    acts = spread(both, plane)
    enc_other = swap(enc_weight, "core")
    dec = (dec_weight, swap(dec_weight, "core"))
    bias = jnp.stack([enc_bias, swap(enc_bias, "core")])[:, None, :]
    far_acts = swap(acts, "core")

    dec_f32 = [d.astype(f32) for d in dec]
    squares = jnp.pad(jnp.stack([jnp.sum(d * d, axis=1) for d in dec_f32]), ((0, 6), (0, 0)))
    total = sum_over_layer([dot(acts, enc_weight), dot(acts, enc_other)], squares)
    preact = total[: count // 2].reshape(2, count // 4, -1) + bias
    dec_norm = jnp.sqrt(total[count // 2 : count // 2 + 2] + norm_eps)
    gating = jax.nn.sigmoid(sharpness * preact)
    latents = gather_over_layer((preact * gating).astype(bf16))

    def decode(half):
        return (dot(half[0], dec[0]) + dot(half[1], dec[1])).astype(bf16)

    part = in_order(decode(latents[0]), decode(latents[1]), lc, 0)
    parts = lax.all_to_all(part.reshape(plane, 2 * rows, features), PLANE, 0, 0, tiled=True)
    part = jnp.sum(parts.astype(f32), axis=0)
    got = swap(part.astype(bf16), "zhi").astype(f32)
    rebuilt = part + jnp.concatenate([got[rows:], got[:rows]], axis=0)
    residual = spread((rebuilt + dec_bias - both.astype(f32)).astype(bf16), plane)

    lat_grad = sum_over_layer([dot(residual, d, ((1,), (1,))) for d in dec])
    lat_grad = lat_grad.reshape(2, count // 4, -1) + sparsity * dec_norm[:, None, :]

    latents = in_order(*latents, lc, 1)
    lat_sums = jnp.sum(latents.astype(f32), axis=1)
    dec_grads = [
        dot(latents[i], residual, ((0,), (0,))) + (sparsity * lat_sums[i] / dec_norm[i])[:, None] * dec_f32[i]
        for i in (0, 1)
    ]
    dec_grad = dec_grads[0] + swap(dec_grads[1].astype(bf16), "core").astype(f32)

    pre_grad = (lat_grad * (gating + sharpness * preact * gating * (1.0 - gating))).astype(bf16)
    pre_grad = jnp.stack([pre_grad[0], swap(pre_grad[1], "core")])
    near_grad, far_grad = gather_over_layer(pre_grad)
    half = count // 2
    all_acts = jnp.stack(
        [jnp.concatenate([a[i * half : (i + 1) * half] for a in (acts, far_acts)]) for i in (0, 1)]
    )

    def encode(index, grad):
        rows = lax.dynamic_index_in_dim(all_acts, index, 0, keepdims=False)
        return dot(rows, grad.reshape(count, -1), ((0,), (0,)))

    enc_grad = encode(1 - lc, far_grad)
    enc_grad = enc_grad + encode(lc, near_grad)
    return (enc_grad.astype(bf16), dec_grad.astype(bf16))


def solution(mesh):
    fine = Mesh(mesh.devices.reshape(2, 2, 2, 4, 2, 4, 2), (*LAYER, *LAT))
    return jax.shard_map(
        local,
        mesh=fine,
        in_specs=(P(LAT, LAYER), P(LAYER, LAT), P(LAT), P(LAT, LAYER), P(LAYER)),
        out_specs=(P(LAYER, LAT), P(LAT, LAYER)),
        check_vma=False,
    )
```

```python
import jax
import jax.numpy as jnp
from jax import lax
from jax.sharding import Mesh
from jax.sharding import PartitionSpec as P

norm_eps = 1e-06
sparsity = 0.5
sharpness = 4.0
bf16, f32 = jnp.bfloat16, jnp.float32

LAYER = ("la", "lb", "lc")
LAT = ("x", "zhi", "y", "core")
PLANE = ("x", "y")
SWAP = ((0, 1), (1, 0))

QUARTER = ("lc", "lb")


def swap(x, axis):
    return lax.ppermute(x, axis, SWAP)


def spread(block, plane):
    blocks = jnp.broadcast_to(block[None], (plane, *block.shape))
    return lax.all_to_all(blocks, PLANE, 0, 0, tiled=True).reshape(-1, block.shape[-1])


def in_order(mine, other, at, axis):
    first = jnp.where(at == 0, mine, other)
    second = jnp.where(at == 0, other, mine)
    return jnp.concatenate([first, second], axis=axis)


def dot(a, b, dims=((1,), (0,))):
    return lax.dot_general(a, b, (dims, ((), ())), preferred_element_type=f32)


def sum_over_layer(sides, tail=None):
    parts = [s.astype(bf16).reshape(4, -1, s.shape[-1]) for s in sides]
    if tail is not None:
        parts.append(jnp.broadcast_to(tail.astype(bf16), (4, *tail.shape)))
    parts = jnp.concatenate(parts, axis=1)
    total = jnp.sum(lax.all_to_all(parts, QUARTER, 0, 0, tiled=True).astype(f32), axis=0)
    return total + swap(total.astype(bf16), "la").astype(f32)


def gather_over_layer(block):
    blocks = jnp.broadcast_to(block[None], (4, *block.shape))
    blocks = lax.all_to_all(blocks, QUARTER, 0, 0, tiled=True)
    return jnp.stack([blocks[:, i].reshape(-1, block.shape[-1]) for i in (0, 1)])


def local(activations, enc_weight, enc_bias, dec_weight, dec_bias):
    rows, features = activations.shape
    plane = lax.axis_size("x") * lax.axis_size("y")
    count = plane * 2 * rows

    both = jnp.concatenate([activations, swap(activations, "zhi")], axis=0)
    acts = spread(both, plane)
    enc_other = swap(enc_weight, "core")
    dec = (dec_weight, swap(dec_weight, "core"))
    bias = jnp.stack([enc_bias, swap(enc_bias, "core")])[:, None, :]
    far_acts = swap(acts, "core")

    dec_f32 = [d.astype(f32) for d in dec]
    squares = jnp.pad(jnp.stack([jnp.sum(d * d, axis=1) for d in dec_f32]), ((0, 6), (0, 0)))
    total = sum_over_layer([dot(acts, enc_weight), dot(acts, enc_other)], squares)
    preact = total[: count // 2].reshape(2, count // 4, -1) + bias
    dec_norm = jnp.sqrt(total[count // 2 : count // 2 + 2] + norm_eps)
    gating = jax.nn.sigmoid(sharpness * preact)
    latents = gather_over_layer((preact * gating).astype(bf16))

    part = (dot(latents[0], dec[0]) + dot(latents[1], dec[1])).astype(bf16)
    parts = lax.all_to_all(part.reshape(plane, 2 * rows, features), PLANE, 0, 0, tiled=True)
    part = jnp.sum(parts.astype(f32), axis=0)
    got = swap(part.astype(bf16), "zhi").astype(f32)
    rebuilt = part + jnp.concatenate([got[rows:], got[:rows]], axis=0)
    residual = spread((rebuilt + dec_bias - both.astype(f32)).astype(bf16), plane)

    lat_grad = sum_over_layer([dot(residual, d, ((1,), (1,))) for d in dec])
    lat_grad = lat_grad.reshape(2, count // 4, -1) + sparsity * dec_norm[:, None, :]

    lat_sums = jnp.sum(latents.astype(f32), axis=1)
    dec_grads = [
        dot(latents[i], residual, ((0,), (0,))) + (sparsity * lat_sums[i] / dec_norm[i])[:, None] * dec_f32[i]
        for i in (0, 1)
    ]
    dec_grad = dec_grads[0] + swap(dec_grads[1].astype(bf16), "core").astype(f32)

    pre_grad = (lat_grad * (gating + sharpness * preact * gating * (1.0 - gating))).astype(bf16)
    core = lax.axis_index("core")
    pre_grad = in_order(pre_grad[:1], pre_grad[1:], core, 0)
    pre_grad = jnp.broadcast_to(pre_grad[None], (4, *pre_grad.shape))
    pre_grad = lax.all_to_all(pre_grad.reshape(8, *pre_grad.shape[2:]), (*QUARTER, "core"), 0, 0, tiled=True)
    rows = in_order(acts.reshape(4, 1, -1, features), far_acts.reshape(4, 1, -1, features), core, 1)
    enc_grad = dot(rows.reshape(-1, features), pre_grad.reshape(2 * count, -1), ((0,), (0,)))
    return (enc_grad.astype(bf16), dec_grad.astype(bf16))


def solution(mesh):
    fine = Mesh(mesh.devices.reshape(2, 2, 2, 4, 2, 4, 2), (*LAYER, *LAT))
    return jax.shard_map(
        local,
        mesh=fine,
        in_specs=(P(LAT, LAYER), P(LAYER, LAT), P(LAT), P(LAT, LAYER), P(LAYER)),
        out_specs=(P(LAYER, LAT), P(LAT, LAYER)),
        check_vma=False,
    )
```

```python
import jax
import jax.numpy as jnp
from jax import lax
from jax.sharding import Mesh
from jax.sharding import PartitionSpec as P

norm_eps = 1e-06
sparsity = 0.5
sharpness = 4.0
bf16, f32 = jnp.bfloat16, jnp.float32

LAYER = ("la", "lb", "lc")
LAT = ("x", "zhi", "y", "core")
PLANE = ("x", "y")
SWAP = ((0, 1), (1, 0))

QUARTER = ("lc", "lb")


def swap(x, axis):
    return lax.ppermute(x, axis, SWAP)


def spread(block, plane):
    blocks = jnp.broadcast_to(block[None], (plane, *block.shape))
    return lax.all_to_all(blocks, PLANE, 0, 0, tiled=True).reshape(-1, block.shape[-1])


def in_order(mine, other, at, axis):
    first = jnp.where(at == 0, mine, other)
    second = jnp.where(at == 0, other, mine)
    return jnp.concatenate([first, second], axis=axis)


def dot(a, b, dims=((1,), (0,))):
    return lax.dot_general(a, b, (dims, ((), ())), preferred_element_type=f32)


def sum_near(sides, tail=None):
    parts = [s.astype(bf16).reshape(4, -1, s.shape[-1]) for s in sides]
    if tail is not None:
        parts.append(jnp.broadcast_to(tail.astype(bf16), (4, *tail.shape)))
    parts = jnp.concatenate(parts, axis=1)
    return jnp.sum(lax.all_to_all(parts, QUARTER, 0, 0, tiled=True).astype(f32), axis=0)


def sum_far(total):
    return total + swap(total.astype(bf16), "la").astype(f32)


def gather_over_layer(block):
    blocks = jnp.broadcast_to(block[None], (4, *block.shape))
    blocks = lax.all_to_all(blocks, QUARTER, 0, 0, tiled=True)
    return jnp.stack([blocks[:, i].reshape(-1, block.shape[-1]) for i in (0, 1)])


def local(activations, enc_weight, enc_bias, dec_weight, dec_bias):
    rows, features = activations.shape
    hidden = dec_weight.shape[0]
    plane = lax.axis_size("x") * lax.axis_size("y")
    count = plane * 2 * rows

    both = jnp.concatenate([activations, swap(activations, "zhi")], axis=0)
    enc_other = swap(enc_weight, "core")
    dec = (dec_weight, swap(dec_weight, "core"))
    dec_f32 = [d.astype(f32) for d in dec]
    square = jnp.broadcast_to(jnp.sum(dec_f32[0] * dec_f32[0], axis=1)[None], (4, hidden)).astype(bf16)
    both, square = lax.optimization_barrier((both, square))
    acts = spread(both, plane)
    near = dot(acts, enc_weight).astype(bf16)
    near, other = lax.optimization_barrier((near, dec[1]))
    other = other.astype(f32)
    other = jnp.broadcast_to(jnp.sum(other * other, axis=1)[None], (4, hidden)).astype(bf16)
    squares = jnp.concatenate([square, other], axis=0)
    bias = jnp.stack([enc_bias, swap(enc_bias, "core")])[:, None, :]

    total = sum_far(sum_near([near, dot(acts, enc_other)], squares))
    preact = total[: count // 2].reshape(2, count // 4, -1) + bias
    dec_norm = jnp.sqrt(total[count // 2 :: 4] + norm_eps)
    gating = jax.nn.sigmoid(sharpness * preact)
    latents = gather_over_layer((preact * gating).astype(bf16))

    part = (dot(latents[0], dec[0]) + dot(latents[1], dec[1])).astype(bf16)
    parts = lax.all_to_all(part.reshape(plane, 2 * rows, features), PLANE, 0, 0, tiled=True)
    part = jnp.sum(parts.astype(f32), axis=0)
    got = swap(part.astype(bf16), "zhi").astype(f32)
    rebuilt = part + jnp.concatenate([got[rows:], got[:rows]], axis=0)
    residual = spread((rebuilt + dec_bias - both.astype(f32)).astype(bf16), plane)

    lat_grad = sum_near([dot(residual, d, ((1,), (1,))) for d in dec])
    lat_grad, latents, acts_later, residual = lax.optimization_barrier((lat_grad, latents, acts, residual))
    far_acts = swap(acts_later, "core")
    lat_grad = sum_far(lat_grad)
    lat_grad = lat_grad.reshape(2, count // 4, -1) + sparsity * dec_norm[:, None, :]

    lat_sums = jnp.sum(latents.astype(f32), axis=1)
    dec_grads = [
        dot(latents[i], residual, ((0,), (0,))) + (sparsity * lat_sums[i] / dec_norm[i])[:, None] * dec_f32[i]
        for i in (0, 1)
    ]
    dec_grad = dec_grads[0] + swap(dec_grads[1].astype(bf16), "core").astype(f32)

    pre_grad = (lat_grad * (gating + sharpness * preact * gating * (1.0 - gating))).astype(bf16)
    core = lax.axis_index("core")
    pre_grad = in_order(pre_grad[:1], pre_grad[1:], core, 0)
    pre_grad = jnp.broadcast_to(pre_grad[None], (4, *pre_grad.shape))
    pre_grad = lax.all_to_all(pre_grad.reshape(8, *pre_grad.shape[2:]), (*QUARTER, "core"), 0, 0, tiled=True)
    rows = in_order(acts.reshape(4, 1, -1, features), far_acts.reshape(4, 1, -1, features), core, 1)
    enc_grad = dot(rows.reshape(-1, features), pre_grad.reshape(2 * count, -1), ((0,), (0,)))
    return (enc_grad.astype(bf16), dec_grad.astype(bf16))


def solution(mesh):
    fine = Mesh(mesh.devices.reshape(2, 2, 2, 4, 2, 4, 2), (*LAYER, *LAT))
    return jax.shard_map(
        local,
        mesh=fine,
        in_specs=(P(LAT, LAYER), P(LAYER, LAT), P(LAT), P(LAT, LAYER), P(LAYER)),
        out_specs=(P(LAYER, LAT), P(LAT, LAYER)),
        check_vma=False,
    )
```

```python
import jax
import jax.numpy as jnp
from jax import lax
from jax.experimental import pallas as pl
from jax.experimental.pallas import tpu as pltpu
from jax.sharding import Mesh
from jax.sharding import PartitionSpec as P

norm_eps = 1e-06
sparsity = 0.5
sharpness = 4.0
bf16, f32 = jnp.bfloat16, jnp.float32

LAYER = ("la", "lb", "lc")
LAT = ("x", "zhi", "y", "core")
PLANE = ("x", "y")
SWAP = ((0, 1), (1, 0))

QUARTER = ("lc", "lb")


def swap(x, axis):
    return lax.ppermute(x, axis, SWAP)


def spread(block, plane):
    blocks = jnp.broadcast_to(block[None], (plane, *block.shape))
    return lax.all_to_all(blocks, PLANE, 0, 0, tiled=True).reshape(-1, block.shape[-1])


def in_order(mine, other, at, axis):
    first = jnp.where(at == 0, mine, other)
    second = jnp.where(at == 0, other, mine)
    return jnp.concatenate([first, second], axis=axis)


def dot(a, b, dims=((1,), (0,))):
    return lax.dot_general(a, b, (dims, ((), ())), preferred_element_type=f32)


def sum_near(sides, tail=None):
    parts = [s.astype(bf16).reshape(4, -1, s.shape[-1]) for s in sides]
    if tail is not None:
        parts.append(jnp.broadcast_to(tail.astype(bf16), (4, *tail.shape)))
    parts = jnp.concatenate(parts, axis=1)
    return jnp.sum(lax.all_to_all(parts, QUARTER, 0, 0, tiled=True).astype(f32), axis=0)


def sum_far(total):
    return total + swap(total.astype(bf16), "la").astype(f32)


def gather_over_layer(block):
    blocks = jnp.broadcast_to(block[None], (4, *block.shape))
    blocks = lax.all_to_all(blocks, QUARTER, 0, 0, tiled=True)
    return jnp.stack([blocks[:, i].reshape(-1, block.shape[-1]) for i in (0, 1)])


def outer_body(rows, grads, out):
    out[...] = lax.dot_general(
        rows[...], grads[...], (((0,), (0,)), ((), ())), preferred_element_type=f32
    ).astype(bf16)


def outer(rows, grads):
    count, features = rows.shape
    tile = features // 3
    return pl.pallas_call(
        outer_body,
        grid=(features // tile,),
        in_specs=[
            pl.BlockSpec((count, tile), lambda i: (0, i)),
            pl.BlockSpec(grads.shape, lambda i: (0, 0)),
        ],
        out_specs=pl.BlockSpec((tile, grads.shape[1]), lambda i: (i, 0)),
        out_shape=jax.ShapeDtypeStruct((features, grads.shape[1]), bf16),
        compiler_params=pltpu.CompilerParams(vmem_limit_bytes=24 * 1024 * 1024),
        cost_estimate=pl.CostEstimate(flops=2 * count * features * grads.shape[1], bytes_accessed=3 << 20, transcendentals=0),
    )(rows, grads)


def local(activations, enc_weight, enc_bias, dec_weight, dec_bias):
    rows, features = activations.shape
    hidden = dec_weight.shape[0]
    plane = lax.axis_size("x") * lax.axis_size("y")
    count = plane * 2 * rows

    both = jnp.concatenate([activations, swap(activations, "zhi")], axis=0)
    enc_other = swap(enc_weight, "core")
    dec = (dec_weight, swap(dec_weight, "core"))
    dec_f32 = [d.astype(f32) for d in dec]
    square = jnp.broadcast_to(jnp.sum(dec_f32[0] * dec_f32[0], axis=1)[None], (4, hidden)).astype(bf16)
    both, square = lax.optimization_barrier((both, square))
    acts = spread(both, plane)
    near = dot(acts, enc_weight).astype(bf16)
    near, other = lax.optimization_barrier((near, dec[1]))
    other = other.astype(f32)
    other = jnp.broadcast_to(jnp.sum(other * other, axis=1)[None], (4, hidden)).astype(bf16)
    squares = jnp.concatenate([square, other], axis=0)
    bias = jnp.stack([enc_bias, swap(enc_bias, "core")])[:, None, :]

    total = sum_far(sum_near([near, dot(acts, enc_other)], squares))
    preact = total[: count // 2].reshape(2, count // 4, -1) + bias
    dec_norm = jnp.sqrt(total[count // 2 :: 4] + norm_eps)
    gating = jax.nn.sigmoid(sharpness * preact)
    latents = gather_over_layer((preact * gating).astype(bf16))

    part = (dot(latents[0], dec[0]) + dot(latents[1], dec[1])).astype(bf16)
    parts = lax.all_to_all(part.reshape(plane, 2 * rows, features), PLANE, 0, 0, tiled=True)
    part = jnp.sum(parts.astype(f32), axis=0)
    got = swap(part.astype(bf16), "zhi").astype(f32)
    rebuilt = part + jnp.concatenate([got[rows:], got[:rows]], axis=0)
    residual = spread((rebuilt + dec_bias - both.astype(f32)).astype(bf16), plane)

    lat_grad = sum_near([dot(residual, d, ((1,), (1,))) for d in dec])
    lat_grad, latents, acts_later, residual = lax.optimization_barrier((lat_grad, latents, acts, residual))
    far_acts = swap(acts_later, "core")
    lat_grad = sum_far(lat_grad)
    lat_grad = lat_grad.reshape(2, count // 4, -1) + sparsity * dec_norm[:, None, :]

    lat_sums = jnp.sum(latents.astype(f32), axis=1)
    dec_grads = [
        dot(latents[i], residual, ((0,), (0,))) + (sparsity * lat_sums[i] / dec_norm[i])[:, None] * dec_f32[i]
        for i in (0, 1)
    ]
    dec_grad = dec_grads[0] + swap(dec_grads[1].astype(bf16), "core").astype(f32)

    pre_grad = (lat_grad * (gating + sharpness * preact * gating * (1.0 - gating))).astype(bf16)
    core = lax.axis_index("core")
    pre_grad = in_order(pre_grad[:1], pre_grad[1:], core, 0)
    pre_grad = jnp.broadcast_to(pre_grad[None], (4, *pre_grad.shape))
    pre_grad = lax.all_to_all(pre_grad.reshape(8, *pre_grad.shape[2:]), (*QUARTER, "core"), 0, 0, tiled=True)
    rows = in_order(acts.reshape(4, 1, -1, features), far_acts.reshape(4, 1, -1, features), core, 1)
    enc_grad = outer(rows.reshape(-1, features), pre_grad.reshape(2 * count, -1))
    return (enc_grad, dec_grad.astype(bf16))


def solution(mesh):
    fine = Mesh(mesh.devices.reshape(2, 2, 2, 4, 2, 4, 2), (*LAYER, *LAT))
    return jax.shard_map(
        local,
        mesh=fine,
        in_specs=(P(LAT, LAYER), P(LAYER, LAT), P(LAT), P(LAT, LAYER), P(LAYER)),
        out_specs=(P(LAYER, LAT), P(LAT, LAYER)),
        check_vma=False,
    )
```

```python
import jax
import jax.numpy as jnp
from jax import lax
from jax.experimental import pallas as pl
from jax.experimental.pallas import tpu as pltpu
from jax.sharding import Mesh
from jax.sharding import PartitionSpec as P

norm_eps = 1e-06
sparsity = 0.5
sharpness = 4.0
bf16, f32 = jnp.bfloat16, jnp.float32

LAYER = ("la", "lb", "lc")
LAT = ("x", "zhi", "y", "core")
PLANE = ("x", "y")
SWAP = ((0, 1), (1, 0))

QUARTER = ("lc", "lb")


def swap(x, axis):
    return lax.ppermute(x, axis, SWAP)


def spread(block, plane):
    blocks = jnp.broadcast_to(block[None], (plane, *block.shape))
    return lax.all_to_all(blocks, PLANE, 0, 0, tiled=True).reshape(-1, block.shape[-1])


def in_order(mine, other, at, axis):
    first = jnp.where(at == 0, mine, other)
    second = jnp.where(at == 0, other, mine)
    return jnp.concatenate([first, second], axis=axis)


def dot(a, b, dims=((1,), (0,))):
    return lax.dot_general(a, b, (dims, ((), ())), preferred_element_type=f32)


def sum_near(sides, tail=None):
    parts = [s.astype(bf16).reshape(4, -1, s.shape[-1]) for s in sides]
    if tail is not None:
        parts.append(jnp.broadcast_to(tail.astype(bf16), (4, *tail.shape)))
    parts = jnp.concatenate(parts, axis=1)
    return jnp.sum(lax.all_to_all(parts, QUARTER, 0, 0, tiled=True).astype(f32), axis=0)


def sum_far(total):
    return total + swap(total.astype(bf16), "la").astype(f32)


def gather_over_layer(block):
    blocks = jnp.broadcast_to(block[None], (4, *block.shape))
    blocks = lax.all_to_all(blocks, QUARTER, 0, 0, tiled=True)
    return jnp.stack([blocks[:, i].reshape(-1, block.shape[-1]) for i in (0, 1)])


def outer_body(rows, grads, out):
    out[...] = lax.dot_general(
        rows[...], grads[...], (((0,), (0,)), ((), ())), preferred_element_type=f32
    ).astype(bf16)


def outer(rows, grads):
    count, features = rows.shape
    tile = features
    return pl.pallas_call(
        outer_body,
        grid=(features // tile,),
        in_specs=[
            pl.BlockSpec((count, tile), lambda i: (0, i)),
            pl.BlockSpec(grads.shape, lambda i: (0, 0)),
        ],
        out_specs=pl.BlockSpec((tile, grads.shape[1]), lambda i: (i, 0)),
        out_shape=jax.ShapeDtypeStruct((features, grads.shape[1]), bf16),
        compiler_params=pltpu.CompilerParams(vmem_limit_bytes=24 * 1024 * 1024),
        cost_estimate=pl.CostEstimate(flops=2 * count * features * grads.shape[1], bytes_accessed=3 << 20, transcendentals=0),
    )(rows, grads)


def local(activations, enc_weight, enc_bias, dec_weight, dec_bias):
    rows, features = activations.shape
    hidden = dec_weight.shape[0]
    plane = lax.axis_size("x") * lax.axis_size("y")
    count = plane * 2 * rows

    both = jnp.concatenate([activations, swap(activations, "zhi")], axis=0)
    enc_other = swap(enc_weight, "core")
    dec = (dec_weight, swap(dec_weight, "core"))
    dec_f32 = [d.astype(f32) for d in dec]
    square = jnp.broadcast_to(jnp.sum(dec_f32[0] * dec_f32[0], axis=1)[None], (4, hidden)).astype(bf16)
    both, square = lax.optimization_barrier((both, square))
    acts = spread(both, plane)
    near = dot(acts, enc_weight).astype(bf16)
    near, other = lax.optimization_barrier((near, dec[1]))
    other = other.astype(f32)
    other = jnp.broadcast_to(jnp.sum(other * other, axis=1)[None], (4, hidden)).astype(bf16)
    squares = jnp.concatenate([square, other], axis=0)
    bias = jnp.stack([enc_bias, swap(enc_bias, "core")])[:, None, :]

    total = sum_far(sum_near([near, dot(acts, enc_other)], squares))
    preact = total[: count // 2].reshape(2, count // 4, -1) + bias
    dec_norm = jnp.sqrt(total[count // 2 :: 4] + norm_eps)
    gating = jax.nn.sigmoid(sharpness * preact)
    latents = gather_over_layer((preact * gating).astype(bf16))

    part = (dot(latents[0], dec[0]) + dot(latents[1], dec[1])).astype(bf16)
    parts = lax.all_to_all(part.reshape(plane, 2 * rows, features), PLANE, 0, 0, tiled=True)
    part = jnp.sum(parts.astype(f32), axis=0)
    got = swap(part.astype(bf16), "zhi").astype(f32)
    rebuilt = part + jnp.concatenate([got[rows:], got[:rows]], axis=0)
    residual = spread((rebuilt + dec_bias - both.astype(f32)).astype(bf16), plane)

    lat_grad = sum_near([dot(residual, d, ((1,), (1,))) for d in dec])
    lat_grad, latents, acts_later, residual = lax.optimization_barrier((lat_grad, latents, acts, residual))
    far_acts = swap(acts_later, "core")
    lat_grad = sum_far(lat_grad)
    lat_grad = lat_grad.reshape(2, count // 4, -1) + sparsity * dec_norm[:, None, :]

    lat_sums = jnp.sum(latents.astype(f32), axis=1)
    dec_grads = [
        dot(latents[i], residual, ((0,), (0,))) + (sparsity * lat_sums[i] / dec_norm[i])[:, None] * dec_f32[i]
        for i in (0, 1)
    ]
    dec_grad = dec_grads[0] + swap(dec_grads[1].astype(bf16), "core").astype(f32)

    pre_grad = (lat_grad * (gating + sharpness * preact * gating * (1.0 - gating))).astype(bf16)
    core = lax.axis_index("core")
    pre_grad = in_order(pre_grad[:1], pre_grad[1:], core, 0)
    pre_grad = jnp.broadcast_to(pre_grad[None], (4, *pre_grad.shape))
    pre_grad = lax.all_to_all(pre_grad.reshape(8, *pre_grad.shape[2:]), (*QUARTER, "core"), 0, 0, tiled=True)
    rows = in_order(acts.reshape(4, 1, -1, features), far_acts.reshape(4, 1, -1, features), core, 1)
    enc_grad = outer(rows.reshape(-1, features), pre_grad.reshape(2 * count, -1))
    return (enc_grad, dec_grad.astype(bf16))


def solution(mesh):
    fine = Mesh(mesh.devices.reshape(2, 2, 2, 4, 2, 4, 2), (*LAYER, *LAT))
    return jax.shard_map(
        local,
        mesh=fine,
        in_specs=(P(LAT, LAYER), P(LAYER, LAT), P(LAT), P(LAT, LAYER), P(LAYER)),
        out_specs=(P(LAYER, LAT), P(LAT, LAYER)),
        check_vma=False,
    )
```
